32 devices in a mesh: groups: 2 (over x), row: 4 (over y, core), col: 4 (over z).
Axes of the slice: x: 2, y: 2, z: 4, core: 2. Of those that a mesh axis runs over, the one named last changes fastest.
Arguments:
- embeddings: float32 [32, 8192], P(None, ('groups', 'row', 'col')), parts along dimension 1, may hold values from -6 to 6
- inv_length: float32 [32], replicated, may hold values from 0.25 to 0.6
- task_cov: float32 [16, 16], replicated, may hold values from -0.1 to 2.4, as said below
- noise: float32 [16], replicated, may hold values from 0.2 to 1
- targets: float32 [16, 8192], P(None, ('groups', 'row', 'col')), parts along dimension 1, may hold values from -25 to 25
Outputs:
- solution_field: float32 [16, 8192], P(None, ('groups', 'row', 'col')), parts along dimension 1
- residual: float32 [16, 8192], P(None, ('groups', 'row', 'col')), parts along dimension 1
The draws below stay inside these ranges and needn't reach their ends.
There are 2 independent parts, one for each index of `groups`. The reference program is written for one: setup_inputs(seed, part) draws one part's arguments, and reference() takes and returns one part's arrays. A program takes and returns all parts, laid end to end along the dimension named above; an argument that names none is the same for every part. Nothing has to cross between parts.
Inputs may be any that keep to these rules, and one draw needn't show every extreme that they name: `task_cov`: symmetric; each diagonal entry exceeds the sum of the magnitudes of the other entries of its row.
All inputs are finite; a program needn't handle non-finite values.
Results may differ from the reference program's by a relative error of at most 0.0003.
Values sent between devices are 32-bit elements; how exact they have to be, the bound alone decides.
A program may use at most 128 MiB of HBM per device.

```python
import math
import jax
import jax.numpy as jnp
from jax import lax

TASKS = 16
EMB = 32
ITERS = 2
NTOTAL = 4096


def draw_task_cov(key, part):
    key = jax.random.fold_in(key, 1)
    first, second = jax.random.split(key)
    off = jax.random.uniform(first, (TASKS, TASKS), jnp.float32, -0.1, 0.1)
    off = 0.5 * (off + off.T)
    ident = jnp.eye(TASKS, dtype=jnp.float32)
    diag = jax.random.uniform(second, (TASKS,), jnp.float32, 1.6, 2.4)
    return off * (1.0 - ident) + diag[None, :] * ident


def draw_targets(key, part):
    key = jax.random.fold_in(key, 2)
    first, second = jax.random.split(key, 2)
    place = jnp.arange(NTOTAL).astype(jnp.float32) / NTOTAL
    base = jax.random.truncated_normal(first, -4.0, 4.0, (TASKS, NTOTAL), jnp.float32)
    rise = jnp.exp(jnp.log(3.0) * (place - 0.5))
    task_scale = jnp.exp(jax.random.uniform(second, (TASKS, 1), jnp.float32, 0.0, jnp.log(3.0)))
    return base * rise[None, :] * task_scale


def levels(key, shape, shards, low, largest):
    def one(position, shards_of):
        draws = jax.random.uniform(jax.random.fold_in(jax.random.fold_in(key, 6), position), (shards_of,), jnp.float32, low / len(shards), largest / len(shards))
        return jnp.repeat(jnp.exp(draws), shape[position] // shards_of).reshape((-1,) + (1,) * (len(shape) - position - 1))

    factor_of = one(*shards[0])
    for cut in shards[1:]:
        factor_of = factor_of * one(*cut)
    return factor_of


def scatter_about(stream_key, shape, deviation, most, cuts=(), kind=jnp.bfloat16):
    values = jax.random.normal(stream_key, shape, jnp.float32) * deviation
    if len(cuts) > 0:
        values = levels(stream_key, shape, cuts, -0.22, 0.18) * values
    return jnp.clip(values, min=-most, max=most).astype(kind)


def setup_inputs(seed: int = 0, part: int = 0) -> dict:
    key_of = jax.random.split(jax.random.key(seed), 6)
    own_keys = jax.random.split(jax.random.fold_in(key_of[5], part), 6)
    return {
        "embeddings": scatter_about(own_keys[0], (EMB, NTOTAL), 1.0, 6.0, ((1, 16),), jnp.float32),
        "inv_length": jnp.clip(jnp.exp(jax.random.uniform(key_of[1], (EMB,), jnp.float32, math.log(0.25), math.log(0.6))), 0.25, 0.6),
        "task_cov": draw_task_cov(jax.random.fold_in(key_of[5], 71), part),
        "noise": jnp.clip(jnp.exp(jax.random.uniform(key_of[3], (TASKS,), jnp.float32, math.log(0.2), math.log(1.0))), 0.2, 1.0),
        "targets": draw_targets(jax.random.fold_in(jax.random.fold_in(key_of[5], part), 71), part),
    }


def kernel_apply(field, scaled, sqnorm, task_cov, noise):
    width = min(1024, NTOTAL)
    count = NTOTAL // width
    block_emb = scaled.reshape(EMB, count, width).transpose(1, 0, 2)
    block_sq = sqnorm.reshape(count, width)

    def one_block(pair):
        emb_block, sq_block = pair
        cross = jnp.einsum("kc,kr->cr", scaled, emb_block, precision=lax.Precision.HIGHEST)
        tile = jnp.exp(-0.5 * (sqnorm[:, None] + sq_block[None, :] - 2.0 * cross))
        return jnp.dot(field, tile, precision=lax.Precision.HIGHEST)

    parts = lax.map(one_block, (block_emb, block_sq))
    coupled = parts.transpose(1, 0, 2).reshape(TASKS, NTOTAL)
    return jnp.dot(task_cov, coupled, precision=lax.Precision.HIGHEST) + noise[:, None] * field


def reference(embeddings, inv_length, task_cov, noise, targets):
    scaled = embeddings * inv_length[:, None]
    sqnorm = jnp.sum(scaled * scaled, axis=0)
    solution_field = jnp.zeros_like(targets)
    residual = targets
    direction = targets
    norm_now = jnp.sum(residual * residual)
    for step in range(ITERS):
        image = kernel_apply(direction, scaled, sqnorm, task_cov, noise)
        alpha = norm_now / jnp.sum(direction * image)
        solution_field = solution_field + alpha * direction
        residual = residual - alpha * image
        if step + 1 < ITERS:
            norm_next = jnp.sum(residual * residual)
            direction = residual + (norm_next / norm_now) * direction
            norm_now = norm_next
    return solution_field, residual
```

```python
import functools
import math

import jax
import jax.numpy as jnp
from jax import lax
from jax.experimental import pallas as pl
from jax.experimental.pallas import tpu as pltpu
from jax.sharding import PartitionSpec as P

MESH = pl.DeviceIdType.MESH
F32 = jnp.float32
BF16 = jnp.bfloat16
ROOT_LOG2E = math.sqrt(1.0 / math.log(2.0))


def partner(me, k, n):
    if n & (n - 1):
        return [(me + k) % n, (me + n - k) % n][: 1 if 2 * k == n else 2]
    other = me
    bit = 1
    while bit <= k:
        if k & bit:
            other = other + bit * (1 - 2 * ((me // bit) % 2))
        bit *= 2
    return [other]


def three_parts(x):
    high = x.astype(BF16)
    rest = x - high.astype(F32)
    mid = rest.astype(BF16)
    low = (rest - mid.astype(F32)).astype(BF16)
    return high, mid, low


def two_parts(x):
    high = x.astype(BF16)
    return jnp.concatenate([high, (x - high.astype(F32)).astype(BF16)], axis=0)


def kernel(nr, nc, e_hbm, len_hbm, cov_hbm, noise_hbm, t_hbm, sol_ref, res_ref,
           len_v, cov_v, noise_v, e_row, e_col, t_row, cov_b, left, right, k_high, k_low, v_row,
           part_out, part_in, cu_row, mix_out, mix_in, scal,
           sem_local, s_er, r_er, s_ec, r_ec, s_t, r_t, s_p, r_p, s_c, r_c, s_m, r_m, s_s, r_s):
    emb, width = e_hbm.shape
    tasks = t_hbm.shape[0]
    row, col = lax.axis_index("row"), lax.axis_index("col")
    rows_to = [partner(row, k, nr) for k in range(nr)]
    cols_to = [partner(col, k, nc) for k in range(nc)]

    barrier = pltpu.get_barrier_semaphore()
    for k in range(1, nc):
        for peer in cols_to[k]:
            pl.semaphore_signal(barrier, inc=1, device_id={"col": peer}, device_id_type=MESH)
    for k in range(1, nr):
        for peer in rows_to[k]:
            pl.semaphore_signal(barrier, inc=1, device_id={"row": peer}, device_id_type=MESH)
    count = sum(len(p) for p in cols_to[1:] + rows_to[1:])

    local = [
        pltpu.make_async_copy(src, dst, sem_local.at[i])
        for i, (src, dst) in enumerate(
            [(e_hbm, e_row.at[0]), (t_hbm, t_row.at[0]), (len_hbm, len_v), (cov_hbm, cov_v), (noise_hbm, noise_v)]
        )
    ]
    for copy in local:
        copy.start()
    pl.semaphore_wait(barrier, count)

    def to_col(src, dst, send, recv, k):
        return pltpu.make_async_remote_copy(
            src_ref=src, dst_ref=dst, send_sem=send.at[k], recv_sem=recv.at[k],
            device_id={"col": cols_to[k][0]}, device_id_type=MESH)

    def to_row(src, dst, send, recv, k):
        return pltpu.make_async_remote_copy(
            src_ref=src, dst_ref=dst, send_sem=send.at[k], recv_sem=recv.at[k],
            device_id={"row": rows_to[k][0]}, device_id_type=MESH)

    sent = []
    ec = {k: to_col(e_hbm, e_col.at[k], s_ec, r_ec, k) for k in range(1, nc)}
    er = {k: to_row(e_hbm, e_row.at[k], s_er, r_er, k) for k in range(1, nr)}
    tr = {k: to_row(t_hbm, t_row.at[k], s_t, r_t, k) for k in range(1, nr)}
    for group in (er, ec, tr):
        for k in group:
            group[k].start()
            sent.append(group[k])

    for copy in local:
        copy.wait()

    def as_column(x, n):
        eye = lax.broadcasted_iota(jnp.int32, (n, n), 0) == lax.broadcasted_iota(jnp.int32, (n, n), 1)
        return jnp.sum(jnp.where(eye, jnp.broadcast_to(x, (n, n)), 0.0), axis=1, keepdims=True)

    scale = as_column(len_v[...], emb) * ROOT_LOG2E
    noise = as_column(noise_v[...], tasks)
    for k in range(tasks):
        cov_b[k] = jnp.broadcast_to(cov_v[:, k : k + 1], (tasks, 128))

    def couple(x):
        halves = []
        for start in range(0, width, 128):
            acc = cov_b[0] * x[0:1, start : start + 128]
            for k in range(1, tasks):
                acc = acc + cov_b[k] * x[k : k + 1, start : start + 128]
            halves.append(acc)
        return jnp.concatenate(halves, axis=1)

    line = lax.broadcasted_iota(jnp.int32, (16, width), 0)
    depth = left.shape[2]

    def features(x):
        scaled = x * scale
        half = -0.5 * jnp.sum(scaled * scaled, axis=0, keepdims=True)
        return three_parts(scaled), [p.astype(F32) for p in three_parts(half)]

    def extra(parts, first):
        rows = jnp.where((line >= 3 - first) & (line < 6 - first), 1.0, 0.0).astype(F32)
        for i, p in enumerate(parts):
            rows = jnp.where(line == first + i, jnp.broadcast_to(p, rows.shape), rows)
        return rows.astype(BF16)

    def fill(used):
        return [jnp.zeros((depth - used, width), BF16)] if depth > used else []

    def left_of(x):
        (h, m, l), q = features(x)
        return jnp.concatenate([h, h, m, m, h, l, extra(q, 0)] + fill(6 * emb + 16), axis=0).T

    def right_of(x):
        (h, m, l), q = features(x)
        return jnp.concatenate([h, m, h, m, l, h, extra(q, 3)] + fill(6 * emb + 16), axis=0)

    def tile(j, i):
        power = jnp.dot(left[i], right[j], preferred_element_type=F32)
        k = jnp.exp2(power)
        high = k.astype(BF16)
        low = (k - high.astype(F32)).astype(BF16)
        k_high[j, i] = high
        k_low[j, i] = low
        return high, low

    def over_rows(body, init):
        if nr <= 4:
            acc = init
            for i in range(nr):
                acc = body(i, acc)
            return acc
        return lax.fori_loop(0, nr, body, init)

    def fold(acc):
        return acc[:tasks] + acc[tasks:]

    def zero():
        return jnp.zeros((2 * tasks, width), F32)

    def apply(j):
        def body(i, acc):
            v = v_row[i]
            acc = acc + jnp.dot(v, k_high[j, i], preferred_element_type=F32)
            return acc + jnp.dot(v, k_low[j, i], preferred_element_type=F32)
        return fold(over_rows(body, zero()))

    def make_and_apply(j):
        def body(i, acc):
            high, low = tile(j, i)
            v = v_row[i]
            acc = acc + jnp.dot(v, high, preferred_element_type=F32)
            return acc + jnp.dot(v, low, preferred_element_type=F32)
        return fold(over_rows(body, zero()))

    right[0] = right_of(e_row[0])
    for i in range(nr):
        if i:
            er[i].wait_recv()
        left[i] = left_of(e_row[i])
        if nr <= 4:
            tile(0, i)
    if nr > 4:
        over_rows(lambda i, acc: (tile(0, i), acc)[1], 0)
    for i in range(nr):
        if i:
            tr[i].wait_recv()
        v_row[i] = two_parts(couple(t_row[i]))

    parts = {}
    for j in range(1, nc):
        ec[j].wait_recv()
        right[j] = right_of(e_col[j])
        part_out[j] = make_and_apply(j)
        parts[j] = to_col(part_out.at[j], part_in.at[j], s_p, r_p, j)
        parts[j].start()
        sent.append(parts[j])
    own = apply(0)
    targets = t_row[0]
    for j in parts:
        parts[j].wait_recv()
        own = own + part_in[j]
    image = own + noise * targets

    def lanes(x):
        total = None
        for r in range(0, tasks, 8):
            for c in range(0, width, 128):
                piece = x[r : r + 8, c : c + 128]
                total = piece if total is None else total + piece
        return total

    cu_row[0, :tasks] = couple(image)
    cu_row[0, tasks:, :128] = lanes(targets * targets)
    cu_row[0, tasks:, 128:] = lanes(targets * image)
    cus = {}
    for k in range(1, nr):
        cus[k] = to_row(cu_row.at[0], cu_row.at[k], s_c, r_c, k)
        cus[k].start()
        sent.append(cus[k])
    v_row[0] = two_parts(cu_row[0, :tasks])
    sums = cu_row[0, tasks:]
    for k in range(1, nr):
        cus[k].wait_recv()
        v_row[k] = two_parts(cu_row[k, :tasks])
        sums = sums + cu_row[k, tasks:]

    mixes = {}
    for j in range(1, nc):
        mix_out[j, :tasks] = apply(j)
        mix_out[j, tasks:] = sums
        mixes[j] = to_col(mix_out.at[j], mix_in.at[j], s_m, r_m, j)
        mixes[j].start()
        sent.append(mixes[j])
    second = apply(0)
    for j in mixes:
        mixes[j].wait_recv()
        second = second + mix_in[j, :tasks]
        sums = sums + mix_in[j, tasks:]
    second = second + noise * image

    def total(x):
        return jnp.sum(jnp.sum(x, axis=1, keepdims=True), axis=0, keepdims=True)

    tt, tu = total(sums[:, :128]), total(sums[:, 128:])
    alpha = tt / tu
    residual = targets - alpha * image
    image_r = image - alpha * second

    rr, ra, ru = (total(lanes(residual * x)) for x in (residual, image_r, image))
    lane = lax.broadcasted_iota(jnp.int32, (1, 128), 1)
    mine = jnp.where(lane == 0, rr, jnp.where(lane == 1, ra, jnp.where(lane == 2, ru, 0.0)))
    scal[0] = mine
    finals = []
    for r in range(nr):
        for c in range(nc):
            k = r * nc + c
            if k:
                copy = pltpu.make_async_remote_copy(
                    src_ref=scal.at[0], dst_ref=scal.at[k], send_sem=s_s.at[k], recv_sem=r_s.at[k],
                    device_id={"row": rows_to[r][0], "col": cols_to[c][0]}, device_id_type=MESH)
                copy.start()
                finals.append((k, copy))
                sent.append(copy)
    for k, copy in finals:
        copy.wait_recv()
        mine = mine + scal[k]

    def pick(i):
        return jnp.sum(jnp.where(lane == i, mine, 0.0), axis=1, keepdims=True)

    rr, ra, ru = pick(0), pick(1), pick(2)
    beta = rr / tt
    direction = residual + beta * targets
    image_d = image_r + beta * image
    alpha2 = rr / (ra + 2.0 * beta * ru + beta * beta * tu)
    sol_ref[...] = alpha * targets + alpha2 * direction
    res_ref[...] = residual - alpha2 * image_d
    for copy in sent:
        copy.wait_send()


def solution(mesh):
    nr, nc = mesh.shape["row"], mesh.shape["col"]

    def on_device(embeddings, inv_length, task_cov, noise, targets):
        emb, width = embeddings.shape
        tasks = targets.shape[0]
        depth = -(-(6 * emb + 16) // 256) * 256
        dma = pltpu.SemaphoreType.DMA
        out = jax.ShapeDtypeStruct((tasks, width), F32)
        tiles = nr * nc * width * width
        return pl.pallas_call(
            functools.partial(kernel, nr, nc),
            out_shape=(out, out),
            in_specs=[pl.BlockSpec(memory_space=pl.ANY)] * 5,
            out_specs=(pl.BlockSpec(memory_space=pltpu.VMEM),) * 2,
            scratch_shapes=[
                pltpu.VMEM((1, emb), F32),
                pltpu.VMEM((tasks, tasks), F32),
                pltpu.VMEM((1, tasks), F32),
                pltpu.VMEM((nr, emb, width), F32),
                pltpu.VMEM((nc, emb, width), F32),
                pltpu.VMEM((nr, tasks, width), F32),
                pltpu.VMEM((tasks, tasks, 128), F32),
                pltpu.VMEM((nr, width, depth), BF16),
                pltpu.VMEM((nc, depth, width), BF16),
                pltpu.VMEM((nc, nr, width, width), BF16),
                pltpu.VMEM((nc, nr, width, width), BF16),
                pltpu.VMEM((nr, 2 * tasks, width), BF16),
                pltpu.VMEM((nc, tasks, width), F32),
                pltpu.VMEM((nc, tasks, width), F32),
                pltpu.VMEM((nr, tasks + 8, width), F32),
                pltpu.VMEM((nc, tasks + 8, width), F32),
                pltpu.VMEM((nc, tasks + 8, width), F32),
                pltpu.VMEM((nr * nc, 1, 128), F32),
                dma((5,)),
                dma((nr,)), dma((nr,)),
                dma((nc,)), dma((nc,)),
                dma((nr,)), dma((nr,)),
                dma((nc,)), dma((nc,)),
                dma((nr,)), dma((nr,)),
                dma((nc,)), dma((nc,)),
                dma((nr * nc,)), dma((nr * nc,)),
            ],
            compiler_params=pltpu.CompilerParams(
                collective_id=0, has_side_effects=True, vmem_limit_bytes=56 * 2**20
            ),
            cost_estimate=pl.CostEstimate(
                flops=2 * tiles * (depth + 8 * tasks), bytes_accessed=4 * width * (emb + 3 * tasks), transcendentals=tiles
            ),
        )(embeddings, inv_length.reshape(1, emb), task_cov, noise.reshape(1, tasks), targets)

    spread = P(None, ("groups", "row", "col"))
    return jax.shard_map(
        on_device,
        mesh=mesh,
        in_specs=(spread, P(), P(), P(), spread),
        out_specs=(spread, spread),
        check_vma=False,
    )
```

```python
import functools
import math

import jax
import jax.numpy as jnp
from jax import lax
from jax.experimental import pallas as pl
from jax.experimental.pallas import tpu as pltpu
from jax.sharding import PartitionSpec as P

MESH = pl.DeviceIdType.MESH
F32 = jnp.float32
BF16 = jnp.bfloat16
ROOT_LOG2E = math.sqrt(1.0 / math.log(2.0))


def partner(me, k, n):
    assert n & (n - 1) == 0
    bit = 1
    while bit <= k:
        if k & bit:
            me = me + bit * (1 - 2 * ((me // bit) % 2))
        bit *= 2
    return me


def three_parts(x):
    high = x.astype(BF16)
    rest = x - high.astype(F32)
    mid = rest.astype(BF16)
    low = (rest - mid.astype(F32)).astype(BF16)
    return high, mid, low


def two_parts(x):
    high = x.astype(BF16)
    return jnp.concatenate([high, (x - high.astype(F32)).astype(BF16)], axis=0)


def kernel(nr, nc, e_hbm, len_hbm, cov_hbm, noise_hbm, t_hbm, out_ref,
           len_v, cov_v, noise_v, e_row, e_col, t_row, t_col, cov_b, left, right, k_high, k_low, v_row,
           acc_row, part_out, part_in, mix_out, mix_in, scal,
           sem_local, s_er, r_er, s_ec, r_ec, s_t, r_t, s_u, r_u, s_p, r_p, s_m, r_m, s_s, r_s):
    emb, width = e_hbm.shape
    tasks = t_hbm.shape[0]
    row, col = lax.axis_index("row"), lax.axis_index("col")
    rows_to = [partner(row, k, nr) for k in range(nr)]
    cols_to = [partner(col, k, nc) for k in range(nc)]

    barrier = pltpu.get_barrier_semaphore()
    for k in range(1, nc):
        pl.semaphore_signal(barrier, inc=1, device_id={"col": cols_to[k]}, device_id_type=MESH)
    for k in range(1, nr):
        pl.semaphore_signal(barrier, inc=1, device_id={"row": rows_to[k]}, device_id_type=MESH)

    local = [
        pltpu.make_async_copy(src, dst, sem_local.at[i])
        for i, (src, dst) in enumerate(
            [(e_hbm, e_row.at[0]), (t_hbm, t_row.at[0]), (len_hbm, len_v), (cov_hbm, cov_v), (noise_hbm, noise_v)]
        )
    ]
    for copy in local:
        copy.start()
    pl.semaphore_wait(barrier, nc + nr - 2)

    def to_col(src, dst, send, recv, k):
        return pltpu.make_async_remote_copy(
            src_ref=src, dst_ref=dst, send_sem=send.at[k], recv_sem=recv.at[k],
            device_id={"col": cols_to[k]}, device_id_type=MESH)

    def to_row(src, dst, send, recv, k):
        return pltpu.make_async_remote_copy(
            src_ref=src, dst_ref=dst, send_sem=send.at[k], recv_sem=recv.at[k],
            device_id={"row": rows_to[k]}, device_id_type=MESH)

    sent = []
    ec = {k: to_col(e_hbm, e_col.at[k], s_ec, r_ec, k) for k in range(1, nc)}
    er = {k: to_row(e_hbm, e_row.at[k], s_er, r_er, k) for k in range(1, nr)}
    tr = {k: to_row(t_hbm, t_row.at[k], s_t, r_t, k) for k in range(1, nr)}
    tc = {k: to_col(t_hbm, t_col.at[k], s_u, r_u, k) for k in range(1, nc)}
    for group in (ec, er, tc, tr):
        for k in reversed(group):
            group[k].start()
            sent.append(group[k])

    for copy in local:
        copy.wait()

    def as_column(x, n):
        eye = lax.broadcasted_iota(jnp.int32, (n, n), 0) == lax.broadcasted_iota(jnp.int32, (n, n), 1)
        return jnp.sum(jnp.where(eye, jnp.broadcast_to(x, (n, n)), 0.0), axis=1, keepdims=True)

    scale = as_column(len_v[...], emb) * ROOT_LOG2E
    noise = as_column(noise_v[...], tasks)
    for k in range(tasks):
        cov_b[k] = jnp.broadcast_to(cov_v[:, k : k + 1], (tasks, 128))

    def couple(x):
        halves = []
        for start in range(0, width, 128):
            acc = cov_b[0] * x[0:1, start : start + 128]
            for k in range(1, tasks):
                acc = acc + cov_b[k] * x[k : k + 1, start : start + 128]
            halves.append(acc)
        return jnp.concatenate(halves, axis=1)

    line = lax.broadcasted_iota(jnp.int32, (16, width), 0)
    depth = left.shape[2]

    def features(x):
        scaled = x * scale
        half = -0.5 * jnp.sum(scaled * scaled, axis=0, keepdims=True)
        return three_parts(scaled), [p.astype(F32) for p in three_parts(half)]

    def extra(parts, first):
        rows = jnp.where((line >= 3 - first) & (line < 6 - first), 1.0, 0.0).astype(F32)
        for i, p in enumerate(parts):
            rows = jnp.where(line == first + i, jnp.broadcast_to(p, rows.shape), rows)
        return rows.astype(BF16)

    def fill(used):
        return [jnp.zeros((depth - used, width), BF16)] if depth > used else []

    def left_of(x):
        (h, m, l), q = features(x)
        return jnp.concatenate([h, h, m, m, h, l, extra(q, 0)] + fill(6 * emb + 16), axis=0).T

    def right_of(x):
        (h, m, l), q = features(x)
        return jnp.concatenate([h, m, h, m, l, h, extra(q, 3)] + fill(6 * emb + 16), axis=0)

    def tile(j, i):
        power = jnp.dot(left[i], right[j], preferred_element_type=F32)
        k = jnp.exp2(power)
        high = k.astype(BF16)
        low = (k - high.astype(F32)).astype(BF16)
        k_high[j, i] = high
        k_low[j, i] = low
        return high, low

    def over_rows(body, init):
        if nr <= 4:
            acc = init
            for i in range(nr):
                acc = body(i, acc)
            return acc
        return lax.fori_loop(0, nr, body, init)

    def fold(acc):
        return acc[:tasks] + acc[tasks:]

    right[0] = right_of(e_row[0])
    for i in range(nr):
        if i:
            er[i].wait_recv()
        left[i] = left_of(e_row[i])
    for j in range(nc):
        if j:
            ec[j].wait_recv()
            right[j] = right_of(e_col[j])
            tc[j].wait_recv()
        v = two_parts(couple(t_col[j] if j else t_row[0]))

        last = j + 1 == nc

        def body(i, carry):
            high, low = tile(j, i)
            across = (((1,), (1,)), ((), ()))
            acc = lax.dot_general(v, high, across, preferred_element_type=F32)
            acc = acc + lax.dot_general(v, low, across, preferred_element_type=F32)
            if j:
                acc = acc + acc_row[i]
            if last:
                part_out[i] = fold(acc)
            else:
                acc_row[i] = acc
            return carry
        if not last:
            over_rows(body, 0)

    pieces = min(nr, 4)
    each = nr // pieces
    parts = []
    for piece in range(pieces):
        for i in range(piece * each, (piece + 1) * each):
            body(i, 0)
        here = pl.ds(piece * each, each)
        for k in reversed(range(1, nr)):
            parts.append(to_row(part_out.at[here], part_in.at[k, here], s_p.at[piece], r_p.at[piece], k))
            parts[-1].start()
    sent += parts

    def apply(j):
        def body(i, acc):
            v = v_row[i]
            acc = acc + jnp.dot(v, k_high[j, i], preferred_element_type=F32)
            return acc + jnp.dot(v, k_low[j, i], preferred_element_type=F32)
        return fold(over_rows(body, jnp.zeros((2 * tasks, width), F32)))

    def lanes(x):
        total = None
        for r in range(0, tasks, 8):
            for c in range(0, width, 128):
                piece = x[r : r + 8, c : c + 128]
                total = piece if total is None else total + piece
        return total

    targets = t_row[0]
    for k in range(1, nr):
        tr[k].wait_recv()
    for copy in parts:
        copy.wait_recv()
    tt = tu = None
    for i in range(nr):
        field = part_out[i]
        for k in range(1, nr):
            field = field + part_in[k, i ^ k]
        field = field + noise * t_row[i]
        if i == 0:
            image = field
        v_row[i] = two_parts(field)
        more_tt, more_tu = lanes(t_row[i] * t_row[i]), lanes(t_row[i] * field)
        tt = more_tt if tt is None else tt + more_tt
        tu = more_tu if tu is None else tu + more_tu
    sums = jnp.concatenate([tt, tu], axis=1)

    mixes = {}
    for j in reversed(range(1, nc)):
        mix_out[j, :tasks] = apply(j)
        mix_out[j, tasks:, :256] = sums
        mixes[j] = to_col(mix_out.at[j], mix_in.at[j], s_m, r_m, j)
        mixes[j].start()
        sent.append(mixes[j])
    second = apply(0)
    for j in mixes:
        mixes[j].wait_recv()
        second = second + mix_in[j, :tasks]
        sums = sums + mix_in[j, tasks:, :256]
    second = couple(second) + noise * image

    def total(x):
        return jnp.sum(jnp.sum(x, axis=1, keepdims=True), axis=0, keepdims=True)

    tt, tu = total(sums[:, :128]), total(sums[:, 128:])
    alpha = tt / tu
    residual = targets - alpha * image
    image_r = image - alpha * second

    rr, ra, ru = (total(lanes(residual * x)) for x in (residual, image_r, image))
    lane = lax.broadcasted_iota(jnp.int32, (1, 128), 1)
    mine = jnp.where(lane == 0, rr, jnp.where(lane == 1, ra, jnp.where(lane == 2, ru, 0.0)))
    scal[0] = mine
    finals = []
    for r in reversed(range(nr)):
        for c in reversed(range(nc)):
            k = r * nc + c
            if k:
                copy = pltpu.make_async_remote_copy(
                    src_ref=scal.at[0], dst_ref=scal.at[k], send_sem=s_s.at[k], recv_sem=r_s.at[k],
                    device_id={"row": rows_to[r], "col": cols_to[c]}, device_id_type=MESH)
                copy.start()
                finals.append((k, copy))
                sent.append(copy)
    for k, copy in finals:
        copy.wait_recv()
        mine = mine + scal[k]

    def pick(i):
        return jnp.sum(jnp.where(lane == i, mine, 0.0), axis=1, keepdims=True)

    rr, ra, ru = pick(0), pick(1), pick(2)
    beta = rr / tt
    direction = residual + beta * targets
    image_d = image_r + beta * image
    alpha2 = rr / (ra + 2.0 * beta * ru + beta * beta * tu)
    out_ref[: tasks] = alpha * targets + alpha2 * direction
    out_ref[tasks :] = residual - alpha2 * image_d
    for copy in sent:
        copy.wait_send()


def solution(mesh):
    nr, nc = mesh.shape["row"], mesh.shape["col"]

    def on_device(embeddings, inv_length, task_cov, noise, targets):
        emb, width = embeddings.shape
        tasks = targets.shape[0]
        depth = -(-(6 * emb + 16) // 256) * 256
        dma = pltpu.SemaphoreType.DMA
        out = jax.ShapeDtypeStruct((tasks, width), F32)
        tiles = nr * nc * width * width
        both = pl.pallas_call(
            functools.partial(kernel, nr, nc),
            out_shape=pltpu.VMEM((2 * tasks, width), F32),
            in_specs=[pl.BlockSpec(memory_space=pl.ANY)] * 5,
            out_specs=pl.BlockSpec(memory_space=pltpu.VMEM),
            scratch_shapes=[
                pltpu.VMEM((1, emb), F32),
                pltpu.VMEM((tasks, tasks), F32),
                pltpu.VMEM((1, tasks), F32),
                pltpu.VMEM((nr, emb, width), F32),
                pltpu.VMEM((nc, emb, width), F32),
                pltpu.VMEM((nr, tasks, width), F32),
                pltpu.VMEM((nc, tasks, width), F32),
                pltpu.VMEM((tasks, tasks, 128), F32),
                pltpu.VMEM((nr, width, depth), BF16),
                pltpu.VMEM((nc, depth, width), BF16),
                pltpu.VMEM((nc, nr, width, width), BF16),
                pltpu.VMEM((nc, nr, width, width), BF16),
                pltpu.VMEM((nr, 2 * tasks, width), BF16),
                pltpu.VMEM((nr, 2 * tasks, width), F32),
                pltpu.VMEM((nr, tasks, width), F32),
                pltpu.VMEM((nr, nr, tasks, width), F32),
                pltpu.VMEM((nc, tasks + 8, width), F32),
                pltpu.VMEM((nc, tasks + 8, width), F32),
                pltpu.VMEM((nr * nc, 1, 128), F32),
                dma((5,)),
                dma((nr,)), dma((nr,)),
                dma((nc,)), dma((nc,)),
                dma((nr,)), dma((nr,)),
                dma((nc,)), dma((nc,)),
                dma((min(nr, 4), nr)), dma((min(nr, 4), nr)),
                dma((nc,)), dma((nc,)),
                dma((nr * nc,)), dma((nr * nc,)),
            ],
            compiler_params=pltpu.CompilerParams(
                collective_id=0, has_side_effects=True, vmem_limit_bytes=56 * 2**20
            ),
            cost_estimate=pl.CostEstimate(
                flops=2 * tiles * (depth + 8 * tasks), bytes_accessed=4 * width * (emb + 3 * tasks), transcendentals=tiles
            ),
        )(embeddings, inv_length.reshape(1, emb), task_cov, noise.reshape(1, tasks), targets)
        return both[:tasks], both[tasks:]

    spread = P(None, ("groups", "row", "col"))
    return jax.shard_map(
        on_device,
        mesh=mesh,
        in_specs=(spread, P(), P(), P(), spread),
        out_specs=(spread, spread),
        check_vma=False,
    )
```

```python
import functools
import math

import jax
import jax.numpy as jnp
from jax import lax
from jax.experimental import pallas as pl
from jax.experimental.pallas import tpu as pltpu
from jax.sharding import PartitionSpec as P

MESH = pl.DeviceIdType.MESH
F32 = jnp.float32
BF16 = jnp.bfloat16
ROOT_LOG2E = math.sqrt(1.0 / math.log(2.0))


def partner(me, k, n):
    assert n & (n - 1) == 0
    bit = 1
    while bit <= k:
        if k & bit:
            me = me + bit * (1 - 2 * ((me // bit) % 2))
        bit *= 2
    return me


def three_parts(x):
    high = x.astype(BF16)
    rest = x - high.astype(F32)
    mid = rest.astype(BF16)
    low = (rest - mid.astype(F32)).astype(BF16)
    return high, mid, low


def two_parts(x):
    high = x.astype(BF16)
    return jnp.concatenate([high, (x - high.astype(F32)).astype(BF16)], axis=0)


def kernel(nr, nc, e_hbm, len_hbm, cov_hbm, noise_hbm, t_hbm, out_ref,
           len_v, cov_v, noise_v, e_row, e_col, t_row, t_col, cov_b, left, right, k_high, k_low, v_row,
           acc_row, row_out, row_in, col_out, col_in, mix_out, mix_in, scal,
           sem_local, s_er, r_er, s_ec, r_ec, s_t, r_t, s_u, r_u, s_p, r_p, s_q, r_q, s_m, r_m, s_s, r_s):
    emb, width = e_hbm.shape
    tasks = t_hbm.shape[0]
    row, col = lax.axis_index("row"), lax.axis_index("col")
    rows_to = [partner(row, k, nr) for k in range(nr)]
    cols_to = [partner(col, k, nc) for k in range(nc)]

    barrier = pltpu.get_barrier_semaphore()
    for k in range(1, nc):
        pl.semaphore_signal(barrier, inc=1, device_id={"col": cols_to[k]}, device_id_type=MESH)
    for k in range(1, nr):
        pl.semaphore_signal(barrier, inc=1, device_id={"row": rows_to[k]}, device_id_type=MESH)

    local = [
        pltpu.make_async_copy(src, dst, sem_local.at[i])
        for i, (src, dst) in enumerate(
            [(e_hbm, e_row.at[0]), (t_hbm, t_row.at[0]), (len_hbm, len_v), (cov_hbm, cov_v), (noise_hbm, noise_v)]
        )
    ]
    for copy in local:
        copy.start()
    pl.semaphore_wait(barrier, nc + nr - 2)

    def to_col(src, dst, send, recv, k):
        return pltpu.make_async_remote_copy(
            src_ref=src, dst_ref=dst, send_sem=send.at[k], recv_sem=recv.at[k],
            device_id={"col": cols_to[k]}, device_id_type=MESH)

    def to_row(src, dst, send, recv, k):
        return pltpu.make_async_remote_copy(
            src_ref=src, dst_ref=dst, send_sem=send.at[k], recv_sem=recv.at[k],
            device_id={"row": rows_to[k]}, device_id_type=MESH)

    sent = []
    ec = {k: to_col(e_hbm, e_col.at[k], s_ec, r_ec, k) for k in range(1, nc)}
    er = {k: to_row(e_hbm, e_row.at[k], s_er, r_er, k) for k in range(1, nr)}
    tr = {k: to_row(t_hbm, t_row.at[k], s_t, r_t, k) for k in range(1, nr)}
    tc = {k: to_col(t_hbm, t_col.at[k], s_u, r_u, k) for k in range(1, nc)}
    for group in (ec, er, tc, tr):
        for k in reversed(group):
            group[k].start()
            sent.append(group[k])

    for copy in local:
        copy.wait()

    def as_column(x, n):
        eye = lax.broadcasted_iota(jnp.int32, (n, n), 0) == lax.broadcasted_iota(jnp.int32, (n, n), 1)
        return jnp.sum(jnp.where(eye, jnp.broadcast_to(x, (n, n)), 0.0), axis=1, keepdims=True)

    scale = as_column(len_v[...], emb) * ROOT_LOG2E
    noise = as_column(noise_v[...], tasks)
    for k in range(tasks):
        cov_b[k] = jnp.broadcast_to(cov_v[:, k : k + 1], (tasks, 128))

    def couple(x):
        halves = []
        for start in range(0, width, 128):
            acc = cov_b[0] * x[0:1, start : start + 128]
            for k in range(1, tasks):
                acc = acc + cov_b[k] * x[k : k + 1, start : start + 128]
            halves.append(acc)
        return jnp.concatenate(halves, axis=1)

    line = lax.broadcasted_iota(jnp.int32, (16, width), 0)
    depth = left.shape[2]

    def features(x):
        scaled = x * scale
        half = -0.5 * jnp.sum(scaled * scaled, axis=0, keepdims=True)
        return three_parts(scaled), [p.astype(F32) for p in three_parts(half)]

    def extra(parts, first):
        rows = jnp.where((line >= 3 - first) & (line < 6 - first), 1.0, 0.0).astype(F32)
        for i, p in enumerate(parts):
            rows = jnp.where(line == first + i, jnp.broadcast_to(p, rows.shape), rows)
        return rows.astype(BF16)

    def fill(used):
        return [jnp.zeros((depth - used, width), BF16)] if depth > used else []

    def left_of(x):
        (h, m, l), q = features(x)
        return jnp.concatenate([h, h, m, m, h, l, extra(q, 0)] + fill(6 * emb + 16), axis=0).T

    def right_of(x):
        (h, m, l), q = features(x)
        return jnp.concatenate([h, m, h, m, l, h, extra(q, 3)] + fill(6 * emb + 16), axis=0)

    def tile(j, i):
        power = jnp.dot(left[i], right[j], preferred_element_type=F32)
        k = jnp.exp2(power)
        high = k.astype(BF16)
        low = (k - high.astype(F32)).astype(BF16)
        k_high[j, i] = high
        k_low[j, i] = low
        return high, low

    def over_rows(body, init):
        if nr <= 4:
            acc = init
            for i in range(nr):
                acc = body(i, acc)
            return acc
        return lax.fori_loop(0, nr, body, init)

    def fold(acc):
        return acc[:tasks] + acc[tasks:]

    right[0] = right_of(e_row[0])
    for i in range(nr):
        if i:
            er[i].wait_recv()
        left[i] = left_of(e_row[i])
    for i in range(nr):
        if i:
            tr[i].wait_recv()
        v_row[i] = two_parts(couple(t_row[i]))
    pieces = min(nr, 4)
    each = nr // pieces
    row_sums, col_sums = [], []
    for j in range(nc):
        if j:
            ec[j].wait_recv()
            right[j] = right_of(e_col[j])
            tc[j].wait_recv()
        v_col = two_parts(couple(t_col[j])) if j else v_row[0]
        last = j + 1 == nc

        def body(i, acc):
            high, low = tile(j, i)
            across = (((1,), (1,)), ((), ()))
            total = lax.dot_general(v_col, high, across, preferred_element_type=F32)
            total = total + lax.dot_general(v_col, low, across, preferred_element_type=F32)
            if j:
                total = total + acc_row[i]
            if last:
                row_out[i] = fold(total)
            else:
                acc_row[i] = total
            v = v_row[i]
            acc = acc + jnp.dot(v, high, preferred_element_type=F32)
            return acc + jnp.dot(v, low, preferred_element_type=F32)

        acc = jnp.zeros((2 * tasks, width), F32)
        if not last:
            acc = over_rows(body, acc)
        else:
            for piece in range(pieces):
                for i in range(piece * each, (piece + 1) * each):
                    acc = body(i, acc)
                here = pl.ds(piece * each, each)
                for k in reversed(range(1, nr)):
                    row_sums.append(to_row(row_out.at[here], row_in.at[k, here], s_p.at[piece], r_p.at[piece], k))
                    row_sums[-1].start()
        col_out[j] = fold(acc)
        for k in reversed(range(1, nc)):
            col_sums.append(to_col(col_out.at[j], col_in.at[k, j], s_q.at[j], r_q.at[j], k))
            col_sums[-1].start()
    sent += row_sums + col_sums

    def lanes(x):
        total = None
        for r in range(0, tasks, 8):
            for c in range(0, width, 128):
                piece = x[r : r + 8, c : c + 128]
                total = piece if total is None else total + piece
        return total

    def total(x):
        return jnp.sum(jnp.sum(x, axis=1, keepdims=True), axis=0, keepdims=True)

    def added(terms):
        return functools.reduce(lambda a, b: a + b, terms)

    for copy in row_sums:
        copy.wait_recv()
    images = []
    for i in range(nr):
        field = added([row_out[i]] + [row_in[k, i ^ k] for k in range(1, nr)]) + noise * t_row[i]
        v_row[i] = two_parts(field)
        images.append(field)

    def apply(j):
        def body(i, acc):
            v = v_row[i]
            acc = acc + jnp.dot(v, k_high[j, i], preferred_element_type=F32)
            return acc + jnp.dot(v, k_low[j, i], preferred_element_type=F32)
        return couple(fold(over_rows(body, jnp.zeros((2 * tasks, width), F32))))

    mixes = {}
    for j in reversed(range(nc)):
        mix_out[j] = apply(j)
        if j:
            mixes[j] = to_col(mix_out.at[j], mix_in.at[j], s_m, r_m, j)
            mixes[j].start()
            sent.append(mixes[j])

    targets, image = t_row[0], images[0]
    tt = total(added([lanes(t_row[i] * t_row[i]) for i in range(nr)]))
    tu = total(added([lanes(t_row[i] * images[i]) for i in range(nr)]))
    about = tt / tu
    near = [t_row[i] - about * images[i] for i in range(nr)]
    rr = total(added([lanes(x * x) for x in near]))
    ru = total(added([lanes(x * u) for x, u in zip(near, images)]))
    uu = total(added([lanes(u * u) for u in images]))

    for copy in col_sums:
        copy.wait_recv()
    xx, xu, ww = [noise * near[0] * near[0]], [2.0 * noise * near[0] * image], [noise * image * image]
    for j in range(nc):
        goal = t_col[j] if j else targets
        field = added([col_out[j]] + [col_in[k, j ^ k] for k in range(1, nc)]) + noise * goal
        x = goal - about * field
        of_u = mix_out[j]
        of_x = col_out[j] - about * of_u
        xx.append(x * of_x)
        xu.append(field * of_x + x * of_u)
        ww.append(field * of_u)
    lane = lax.broadcasted_iota(jnp.int32, (1, 128), 1)
    mine = jnp.zeros((1, 128), F32)
    values = [total(lanes(added(terms))) for terms in (xx, xu, ww)] + [about, tt, tu, rr, ru, uu]
    for place, value in enumerate(values):
        mine = jnp.where(lane == place, value, mine)
    scal[0] = mine
    finals = []
    for r in reversed(range(nr)):
        for c in reversed(range(nc)):
            k = r * nc + c
            if k:
                copy = pltpu.make_async_remote_copy(
                    src_ref=scal.at[0], dst_ref=scal.at[k], send_sem=s_s.at[k], recv_sem=r_s.at[k],
                    device_id={"row": rows_to[r], "col": cols_to[c]}, device_id_type=MESH)
                copy.start()
                finals.append((k, copy))
                sent.append(copy)

    second = mix_out[0] + noise * image
    for j in mixes:
        mixes[j].wait_recv()
        second = second + mix_in[j]

    count = nr * nc
    place = lax.broadcasted_iota(jnp.int32, (count, 128), 0)
    table = jnp.broadcast_to(mine, (count, 128))
    for k, copy in finals:
        copy.wait_recv()
        table = jnp.where(place == k, jnp.broadcast_to(scal[k], (count, 128)), table)
    lane = lax.broadcasted_iota(jnp.int32, (count, 128), 1)

    tt = total(jnp.where(lane == 4, table, 0.0)) * (1.0 / nr)
    tu = total(jnp.where(lane == 5, table, 0.0)) * (1.0 / nr)
    alpha = tt / tu
    shift = alpha - jnp.sum(jnp.where(lane == 3, table, 0.0), axis=1, keepdims=True)

    def moved(first, weights):
        factor = jnp.zeros((count, 128), F32)
        for i, weight in enumerate(weights):
            factor = jnp.where(lane == first + i, weight, factor)
        return total(factor * table)

    ra = moved(0, [jnp.ones_like(shift), -shift, shift * shift])
    rr = moved(6, [jnp.ones_like(shift), -2.0 * shift, shift * shift]) * (1.0 / nr)
    ru = moved(7, [jnp.ones_like(shift), -shift]) * (1.0 / nr)

    residual = targets - alpha * image
    image_r = image - alpha * second
    beta = rr / tt
    direction = residual + beta * targets
    image_d = image_r + beta * image
    alpha2 = rr / (ra + 2.0 * beta * ru + beta * beta * tu)
    out_ref[: tasks] = alpha * targets + alpha2 * direction
    out_ref[tasks :] = residual - alpha2 * image_d
    for copy in sent:
        copy.wait_send()


def solution(mesh):
    nr, nc = mesh.shape["row"], mesh.shape["col"]

    def on_device(embeddings, inv_length, task_cov, noise, targets):
        emb, width = embeddings.shape
        tasks = targets.shape[0]
        depth = -(-(6 * emb + 16) // 256) * 256
        dma = pltpu.SemaphoreType.DMA
        out = jax.ShapeDtypeStruct((tasks, width), F32)
        tiles = nr * nc * width * width
        both = pl.pallas_call(
            functools.partial(kernel, nr, nc),
            out_shape=pltpu.VMEM((2 * tasks, width), F32),
            in_specs=[pl.BlockSpec(memory_space=pl.ANY)] * 5,
            out_specs=pl.BlockSpec(memory_space=pltpu.VMEM),
            scratch_shapes=[
                pltpu.VMEM((1, emb), F32),
                pltpu.VMEM((tasks, tasks), F32),
                pltpu.VMEM((1, tasks), F32),
                pltpu.VMEM((nr, emb, width), F32),
                pltpu.VMEM((nc, emb, width), F32),
                pltpu.VMEM((nr, tasks, width), F32),
                pltpu.VMEM((nc, tasks, width), F32),
                pltpu.VMEM((tasks, tasks, 128), F32),
                pltpu.VMEM((nr, width, depth), BF16),
                pltpu.VMEM((nc, depth, width), BF16),
                pltpu.VMEM((nc, nr, width, width), BF16),
                pltpu.VMEM((nc, nr, width, width), BF16),
                pltpu.VMEM((nr, 2 * tasks, width), BF16),
                pltpu.VMEM((nr, 2 * tasks, width), F32),
                pltpu.VMEM((nr, tasks, width), F32),
                pltpu.VMEM((nr, nr, tasks, width), F32),
                pltpu.VMEM((nc, tasks, width), F32),
                pltpu.VMEM((nc, nc, tasks, width), F32),
                pltpu.VMEM((nc, tasks, width), F32),
                pltpu.VMEM((nc, tasks, width), F32),
                pltpu.VMEM((nr * nc, 1, 128), F32),
                dma((5,)),
                dma((nr,)), dma((nr,)),
                dma((nc,)), dma((nc,)),
                dma((nr,)), dma((nr,)),
                dma((nc,)), dma((nc,)),
                dma((min(nr, 4), nr)), dma((min(nr, 4), nr)),
                dma((nc, nc)), dma((nc, nc)),
                dma((nc,)), dma((nc,)),
                dma((nr * nc,)), dma((nr * nc,)),
            ],
            compiler_params=pltpu.CompilerParams(
                collective_id=0, has_side_effects=True, vmem_limit_bytes=56 * 2**20
            ),
            cost_estimate=pl.CostEstimate(
                flops=2 * tiles * (depth + 8 * tasks), bytes_accessed=4 * width * (emb + 3 * tasks), transcendentals=tiles
            ),
        )(embeddings, inv_length.reshape(1, emb), task_cov, noise.reshape(1, tasks), targets)
        return both[:tasks], both[tasks:]

    spread = P(None, ("groups", "row", "col"))
    return jax.shard_map(
        on_device,
        mesh=mesh,
        in_specs=(spread, P(), P(), P(), spread),
        out_specs=(spread, spread),
        check_vma=False,
    )
```

```python
import functools
import math

import jax
import jax.numpy as jnp
from jax import lax
from jax.experimental import pallas as pl
from jax.experimental.pallas import tpu as pltpu
from jax.sharding import PartitionSpec as P

MESH = pl.DeviceIdType.MESH
F32 = jnp.float32
BF16 = jnp.bfloat16
ROOT_LOG2E = math.sqrt(1.0 / math.log(2.0))


def partner(me, k, n):
    assert n & (n - 1) == 0
    bit = 1
    while bit <= k:
        if k & bit:
            me = me + bit * (1 - 2 * ((me // bit) % 2))
        bit *= 2
    return me


def three_parts(x):
    high = x.astype(BF16)
    rest = x - high.astype(F32)
    mid = rest.astype(BF16)
    low = (rest - mid.astype(F32)).astype(BF16)
    return high, mid, low


def two_parts(x):
    high = x.astype(BF16)
    return jnp.concatenate([high, (x - high.astype(F32)).astype(BF16)], axis=0)


def kernel(nr, nc, e_hbm, len_hbm, cov_hbm, noise_hbm, t_hbm, out_ref,
           len_v, cov_v, noise_v, e_row, e_col, t_row, t_col, cov_b, left, right, k_high, k_low, v_row,
           acc_row, row_out, row_in, col_out, col_in, mix_out, mix_in, scal,
           sem_local, s_er, r_er, s_ec, r_ec, s_t, r_t, s_u, r_u, s_p, r_p, s_q, r_q, s_m, r_m, s_s, r_s):
    emb, width = e_hbm.shape
    tasks = t_hbm.shape[0]
    row, col = lax.axis_index("row"), lax.axis_index("col")
    rows_to = [partner(row, k, nr) for k in range(nr)]
    cols_to = [partner(col, k, nc) for k in range(nc)]

    barrier = pltpu.get_barrier_semaphore()
    for k in range(1, nc):
        pl.semaphore_signal(barrier, inc=1, device_id={"col": cols_to[k]}, device_id_type=MESH)
    for k in range(1, nr):
        pl.semaphore_signal(barrier, inc=1, device_id={"row": rows_to[k]}, device_id_type=MESH)

    local = [
        pltpu.make_async_copy(src, dst, sem_local.at[i])
        for i, (src, dst) in enumerate(
            [(e_hbm, e_row.at[0]), (t_hbm, t_row.at[0]), (len_hbm, len_v), (cov_hbm, cov_v), (noise_hbm, noise_v)]
        )
    ]
    for copy in local:
        copy.start()
    pl.semaphore_wait(barrier, nc + nr - 2)

    def to_col(src, dst, send, recv, k):
        return pltpu.make_async_remote_copy(
            src_ref=src, dst_ref=dst, send_sem=send.at[k], recv_sem=recv.at[k],
            device_id={"col": cols_to[k]}, device_id_type=MESH)

    def to_row(src, dst, send, recv, k):
        return pltpu.make_async_remote_copy(
            src_ref=src, dst_ref=dst, send_sem=send.at[k], recv_sem=recv.at[k],
            device_id={"row": rows_to[k]}, device_id_type=MESH)

    for copy in local[:2]:
        copy.wait()
    sent = []
    ec = {k: to_col(e_row.at[0], e_col.at[k], s_ec, r_ec, k) for k in range(1, nc)}
    er = {k: to_row(e_row.at[0], e_row.at[k], s_er, r_er, k) for k in range(1, nr)}
    tr = {k: to_row(t_row.at[0], t_row.at[k], s_t, r_t, k) for k in range(1, nr)}
    tc = {k: to_col(t_row.at[0], t_col.at[k], s_u, r_u, k) for k in range(1, nc)}
    for group in (ec, er, tc, tr):
        for k in reversed(group):
            group[k].start()
            sent.append(group[k])

    for copy in local[2:]:
        copy.wait()

    def as_column(x, n):
        eye = lax.broadcasted_iota(jnp.int32, (n, n), 0) == lax.broadcasted_iota(jnp.int32, (n, n), 1)
        return jnp.sum(jnp.where(eye, jnp.broadcast_to(x, (n, n)), 0.0), axis=1, keepdims=True)

    scale = as_column(len_v[...], emb) * ROOT_LOG2E
    noise = as_column(noise_v[...], tasks)
    for k in range(tasks):
        cov_b[k] = jnp.broadcast_to(cov_v[:, k : k + 1], (tasks, 128))

    def couple(x):
        halves = []
        for start in range(0, width, 128):
            acc = cov_b[0] * x[0:1, start : start + 128]
            for k in range(1, tasks):
                acc = acc + cov_b[k] * x[k : k + 1, start : start + 128]
            halves.append(acc)
        return jnp.concatenate(halves, axis=1)

    line = lax.broadcasted_iota(jnp.int32, (16, width), 0)
    depth = left.shape[2]

    def features(x):
        scaled = x * scale
        half = -0.5 * jnp.sum(scaled * scaled, axis=0, keepdims=True)
        return three_parts(scaled), [p.astype(F32) for p in three_parts(half)]

    def extra(parts, first):
        rows = jnp.where((line >= 3 - first) & (line < 6 - first), 1.0, 0.0).astype(F32)
        for i, p in enumerate(parts):
            rows = jnp.where(line == first + i, jnp.broadcast_to(p, rows.shape), rows)
        return rows.astype(BF16)

    def fill(used):
        return [jnp.zeros((depth - used, width), BF16)] if depth > used else []

    def left_of(x):
        (h, m, l), q = features(x)
        return jnp.concatenate([h, h, m, m, h, l, extra(q, 0)] + fill(6 * emb + 16), axis=0).T

    def right_of(x):
        (h, m, l), q = features(x)
        return jnp.concatenate([h, m, h, m, l, h, extra(q, 3)] + fill(6 * emb + 16), axis=0)

    def tile(j, i):
        power = jnp.dot(left[i], right[j], preferred_element_type=F32)
        k = jnp.exp2(power)
        high = k.astype(BF16)
        low = (k - high.astype(F32)).astype(BF16)
        k_high[j, i] = high
        k_low[j, i] = low
        return high, low

    def over_rows(body, init):
        if nr <= 4:
            acc = init
            for i in range(nr):
                acc = body(i, acc)
            return acc
        return lax.fori_loop(0, nr, body, init)

    def fold(acc):
        return acc[:tasks] + acc[tasks:]

    right[0] = right_of(e_row[0])
    for i in range(nr):
        if i:
            er[i].wait_recv()
        left[i] = left_of(e_row[i])
    for i in range(nr):
        if i:
            tr[i].wait_recv()
        v_row[i] = two_parts(couple(t_row[i]))
    pieces = min(nr, 4)
    each = nr // pieces
    row_sums, col_sums = [], []
    for j in range(nc):
        if j:
            ec[j].wait_recv()
            right[j] = right_of(e_col[j])
        last = j + 1 == nc

        def ahead(i, acc):
            high, low = tile(j, i)
            v = v_row[i]
            acc = acc + jnp.dot(v, high, preferred_element_type=F32)
            return acc + jnp.dot(v, low, preferred_element_type=F32)

        col_out[j] = fold(over_rows(ahead, jnp.zeros((2 * tasks, width), F32)))
        for k in reversed(range(1, nc)):
            col_sums.append(to_col(col_out.at[j], col_in.at[k, j], s_q.at[j], r_q.at[j], k))
            col_sums[-1].start()
        if j:
            tc[j].wait_recv()
        v_col = two_parts(couple(t_col[j])) if j else v_row[0]

        def across(i, carry):
            both = (((1,), (1,)), ((), ()))
            total = lax.dot_general(v_col, k_high[j, i], both, preferred_element_type=F32)
            total = total + lax.dot_general(v_col, k_low[j, i], both, preferred_element_type=F32)
            if j:
                total = total + acc_row[i]
            if last:
                row_out[i] = fold(total)
            else:
                acc_row[i] = total
            return carry

        if not last:
            over_rows(across, 0)
            continue
        for piece in range(pieces):
            for i in range(piece * each, (piece + 1) * each):
                across(i, 0)
            here = pl.ds(piece * each, each)
            for k in reversed(range(1, nr)):
                row_sums.append(to_row(row_out.at[here], row_in.at[k, here], s_p.at[piece], r_p.at[piece], k))
                row_sums[-1].start()
    sent += row_sums + col_sums

    def lanes(x):
        total = None
        for r in range(0, tasks, 8):
            for c in range(0, width, 128):
                piece = x[r : r + 8, c : c + 128]
                total = piece if total is None else total + piece
        return total

    def total(x):
        return jnp.sum(jnp.sum(x, axis=1, keepdims=True), axis=0, keepdims=True)

    def added(terms):
        return functools.reduce(lambda a, b: a + b, terms)

    for copy in row_sums:
        copy.wait_recv()
    images = []
    for i in range(nr):
        field = added([row_out[i]] + [row_in[k, i ^ k] for k in range(1, nr)]) + noise * t_row[i]
        v_row[i] = two_parts(field)
        images.append(field)

    def apply(j):
        def body(i, acc):
            v = v_row[i]
            acc = acc + jnp.dot(v, k_high[j, i], preferred_element_type=F32)
            return acc + jnp.dot(v, k_low[j, i], preferred_element_type=F32)
        return couple(fold(over_rows(body, jnp.zeros((2 * tasks, width), F32))))

    mixes = {}
    for j in reversed(range(nc)):
        mix_out[j] = apply(j)
        if j:
            mixes[j] = to_col(mix_out.at[j], mix_in.at[j], s_m, r_m, j)
            mixes[j].start()
            sent.append(mixes[j])

    targets, image = t_row[0], images[0]
    tt = total(added([lanes(t_row[i] * t_row[i]) for i in range(nr)]))
    tu = total(added([lanes(t_row[i] * images[i]) for i in range(nr)]))
    about = tt / tu
    near = [t_row[i] - about * images[i] for i in range(nr)]
    rr = total(added([lanes(x * x) for x in near]))
    ru = total(added([lanes(x * u) for x, u in zip(near, images)]))
    uu = total(added([lanes(u * u) for u in images]))

    for copy in col_sums:
        copy.wait_recv()
    xx, xu, ww = [noise * near[0] * near[0]], [2.0 * noise * near[0] * image], [noise * image * image]
    for j in range(nc):
        goal = t_col[j] if j else targets
        field = added([col_out[j]] + [col_in[k, j ^ k] for k in range(1, nc)]) + noise * goal
        x = goal - about * field
        of_u = mix_out[j]
        of_x = col_out[j] - about * of_u
        xx.append(x * of_x)
        xu.append(field * of_x + x * of_u)
        ww.append(field * of_u)
    lane = lax.broadcasted_iota(jnp.int32, (1, 128), 1)
    mine = jnp.zeros((1, 128), F32)
    values = [total(lanes(added(terms))) for terms in (xx, xu, ww)] + [about, tt, tu, rr, ru, uu]
    for place, value in enumerate(values):
        mine = jnp.where(lane == place, value, mine)
    scal[0] = mine
    finals = []
    for r in reversed(range(nr)):
        for c in reversed(range(nc)):
            k = r * nc + c
            if k:
                copy = pltpu.make_async_remote_copy(
                    src_ref=scal.at[0], dst_ref=scal.at[k], send_sem=s_s.at[k], recv_sem=r_s.at[k],
                    device_id={"row": rows_to[r], "col": cols_to[c]}, device_id_type=MESH)
                copy.start()
                finals.append((k, copy))
                sent.append(copy)

    second = mix_out[0] + noise * image
    for j in mixes:
        mixes[j].wait_recv()
        second = second + mix_in[j]

    count = nr * nc
    place = lax.broadcasted_iota(jnp.int32, (count, 128), 0)
    table = jnp.broadcast_to(mine, (count, 128))
    for k, copy in finals:
        copy.wait_recv()
        table = jnp.where(place == k, jnp.broadcast_to(scal[k], (count, 128)), table)
    lane = lax.broadcasted_iota(jnp.int32, (count, 128), 1)

    tt = total(jnp.where(lane == 4, table, 0.0)) * (1.0 / nr)
    tu = total(jnp.where(lane == 5, table, 0.0)) * (1.0 / nr)
    alpha = tt / tu
    shift = alpha - jnp.sum(jnp.where(lane == 3, table, 0.0), axis=1, keepdims=True)

    def moved(first, weights):
        factor = jnp.zeros((count, 128), F32)
        for i, weight in enumerate(weights):
            factor = jnp.where(lane == first + i, weight, factor)
        return total(factor * table)

    ra = moved(0, [jnp.ones_like(shift), -shift, shift * shift])
    rr = moved(6, [jnp.ones_like(shift), -2.0 * shift, shift * shift]) * (1.0 / nr)
    ru = moved(7, [jnp.ones_like(shift), -shift]) * (1.0 / nr)

    residual = targets - alpha * image
    image_r = image - alpha * second
    beta = rr / tt
    direction = residual + beta * targets
    image_d = image_r + beta * image
    alpha2 = rr / (ra + 2.0 * beta * ru + beta * beta * tu)
    out_ref[: tasks] = alpha * targets + alpha2 * direction
    out_ref[tasks :] = residual - alpha2 * image_d
    for copy in sent:
        copy.wait_send()


def solution(mesh):
    nr, nc = mesh.shape["row"], mesh.shape["col"]

    def on_device(embeddings, inv_length, task_cov, noise, targets):
        emb, width = embeddings.shape
        tasks = targets.shape[0]
        depth = -(-(6 * emb + 16) // 256) * 256
        dma = pltpu.SemaphoreType.DMA
        out = jax.ShapeDtypeStruct((tasks, width), F32)
        tiles = nr * nc * width * width
        both = pl.pallas_call(
            functools.partial(kernel, nr, nc),
            out_shape=pltpu.VMEM((2 * tasks, width), F32),
            in_specs=[pl.BlockSpec(memory_space=pl.ANY)] * 5,
            out_specs=pl.BlockSpec(memory_space=pltpu.VMEM),
            scratch_shapes=[
                pltpu.VMEM((1, emb), F32),
                pltpu.VMEM((tasks, tasks), F32),
                pltpu.VMEM((1, tasks), F32),
                pltpu.VMEM((nr, emb, width), F32),
                pltpu.VMEM((nc, emb, width), F32),
                pltpu.VMEM((nr, tasks, width), F32),
                pltpu.VMEM((nc, tasks, width), F32),
                pltpu.VMEM((tasks, tasks, 128), F32),
                pltpu.VMEM((nr, width, depth), BF16),
                pltpu.VMEM((nc, depth, width), BF16),
                pltpu.VMEM((nc, nr, width, width), BF16),
                pltpu.VMEM((nc, nr, width, width), BF16),
                pltpu.VMEM((nr, 2 * tasks, width), BF16),
                pltpu.VMEM((nr, 2 * tasks, width), F32),
                pltpu.VMEM((nr, tasks, width), F32),
                pltpu.VMEM((nr, nr, tasks, width), F32),
                pltpu.VMEM((nc, tasks, width), F32),
                pltpu.VMEM((nc, nc, tasks, width), F32),
                pltpu.VMEM((nc, tasks, width), F32),
                pltpu.VMEM((nc, tasks, width), F32),
                pltpu.VMEM((nr * nc, 1, 128), F32),
                dma((5,)),
                dma((nr,)), dma((nr,)),
                dma((nc,)), dma((nc,)),
                dma((nr,)), dma((nr,)),
                dma((nc,)), dma((nc,)),
                dma((min(nr, 4), nr)), dma((min(nr, 4), nr)),
                dma((nc, nc)), dma((nc, nc)),
                dma((nc,)), dma((nc,)),
                dma((nr * nc,)), dma((nr * nc,)),
            ],
            compiler_params=pltpu.CompilerParams(
                collective_id=0, has_side_effects=True, vmem_limit_bytes=56 * 2**20
            ),
            cost_estimate=pl.CostEstimate(
                flops=2 * tiles * (depth + 8 * tasks), bytes_accessed=4 * width * (emb + 3 * tasks), transcendentals=tiles
            ),
        )(embeddings, inv_length.reshape(1, emb), task_cov, noise.reshape(1, tasks), targets)
        return both[:tasks], both[tasks:]

    spread = P(None, ("groups", "row", "col"))
    return jax.shard_map(
        on_device,
        mesh=mesh,
        in_specs=(spread, P(), P(), P(), spread),
        out_specs=(spread, spread),
        check_vma=False,
    )
```
